32 devices in a mesh: row: 4 (over z), slab: 4 (over y, x), rep: 2 (over core).
Axes of the slice: x: 2, y: 2, z: 4, core: 2. Of those that a mesh axis runs over, the one named last changes fastest.
Arguments:
- t2_stored: float32 [2048, 40960], P('row', ('slab', 'rep')), may hold values from -6 to 6
- v_slab: float32 [1536, 40960], P('rep', 'slab'), may hold values from -0.03125 to 0.03125
- block_source: int32 [320], replicated, may hold values from 0 to 319, as said below
- r_in: float32 [2048, 1536], P(('row', 'slab'), 'rep'), may hold values from -6 to 6
Outputs:
- r_out: float32 [2048, 1536], P(('row', 'slab'), 'rep')
The draws below stay inside these ranges and needn't reach their ends.
Inputs may be any that keep to these rules, and one draw needn't show every extreme that they name: block_source is a permutation of the 320 stored blocks. Slab index t owns the blocks k with k // 80 == t; stored block q lies on the device of slab and rep numbered q // 40. Every such device stores either none or exactly 10 blocks owned by any one slab index, and the slab indices it stores blocks for form a run of 4 consecutive indices counted modulo the slab axis.
All inputs are finite; a program needn't handle non-finite values.
Results may differ from the reference program's by a relative error of at most 0.000084.
Values sent between devices are 32-bit elements; how exact they have to be, the bound alone decides.
No kernel may reach another device: no remote copies, remote signals or barrier semaphores. Data moves between devices by JAX's collectives and lax.ppermute only.
A program may use at most 128 MiB of HBM per device.

```python
import jax
import jax.numpy as jnp
from jax import lax

IJ_DEV = 512
AB = 1536
CD = 40960
BLK = 128
NIJ = 2048
NBLK = 320
STORED = 40
CAP = 10
N_ROW = 4
N_SLAB = 4
N_REP = 2


def draw_block_source(key, part):
    key = jax.random.fold_in(key, 7)
    key_start, key_local, key_order = jax.random.split(key, 3)
    holders = N_SLAB * N_REP
    starts = jax.random.permutation(key_start, holders).astype(jnp.int32) % N_SLAB
    places = jnp.arange(STORED, dtype=jnp.int32)
    scores = jax.random.randint(key_local, (holders, STORED), 0, 1 << 20) * STORED + places[None, :]
    shuffle = jnp.argsort(scores, axis=1, stable=True).astype(jnp.int32)
    owners = (starts[:, None] + shuffle // CAP) % N_SLAB
    owners = owners.reshape(NBLK)
    mixing = jax.random.permutation(key_order, NBLK).astype(jnp.int32)
    order_key = owners * NBLK + mixing
    return jnp.argsort(order_key, stable=True).astype(jnp.int32)


def level_of(key, extent, shards, low, high):
    def one(dim, parts):
        draws = jax.random.uniform(jax.random.fold_in(jax.random.fold_in(key, 6), dim), (parts,), jnp.float32, low / len(shards), high / len(shards))
        return jnp.repeat(jnp.exp(draws), extent[dim] // parts).reshape((-1,) + (1,) * (len(extent) - dim - 1))

    factor_of = one(*shards[0])
    for cut in shards[1:]:
        factor_of = factor_of * one(*cut)
    return factor_of


def gaussian(own_key, dims, width, bound, cuts=(), held_as=jnp.bfloat16):
    entries = width * jax.random.normal(own_key, dims, jnp.float32)
    if cuts:
        entries = entries * level_of(own_key, dims, cuts, -0.22, 0.18)
    return jnp.clip(entries, -bound, bound).astype(held_as)


def setup_inputs(seed: int = 0) -> dict:
    key_of = jax.random.split(jax.random.key(seed), 5)
    return {
        "t2_stored": gaussian(key_of[0], (NIJ, CD), 1.0, 6.0, ((0, 4), (1, 8)), jnp.float32),
        "v_slab": gaussian(key_of[1], (AB, CD), CD ** -0.5, 0.03125, ((0, 2), (1, 4)), jnp.float32),
        "block_source": draw_block_source(jax.random.fold_in(key_of[4], 71), 0),
        "r_in": gaussian(key_of[3], (NIJ, AB), 1.0, 6.0, ((0, 16), (1, 2)), jnp.float32),
    }


def reference(t2_stored, v_slab, block_source, r_in):
    def ladder_rows(slab_rows):
        blocked = slab_rows.reshape(IJ_DEV, NBLK, BLK)
        ordered = jnp.take(blocked, block_source.astype(jnp.int32), axis=1).reshape(IJ_DEV, CD)
        return lax.dot_general(ordered, v_slab, (((1,), (1,)), ((), ())),
                               precision=lax.Precision.HIGHEST,
                               preferred_element_type=jnp.float32)

    ladder = lax.map(ladder_rows, t2_stored.reshape(N_ROW, IJ_DEV, CD)).reshape(NIJ, AB)
    return r_in + ladder
```

```python
import jax
import jax.numpy as jnp
from jax import lax
from jax.experimental import pallas as pl
from jax.experimental.pallas import tpu as pltpu
from jax.sharding import PartitionSpec as P

BLK = 128
CHUNK = 2
COST = 20
SPLIT = 5
PART_COST = (20, 4)
DEPTH = 4
VMEM_LIMIT = 30 * 1024 * 1024


def slot_tables(block_source, stored, blk_dev, cap, slabs, reps, slab, rep):
    nblk = block_source.shape[0]
    k = jnp.arange(nblk, dtype=jnp.int32)
    holder = block_source // stored
    owner = k // blk_dev
    key = owner * (slabs * reps) + holder
    earlier = (key[None, :] == key[:, None]) & (k[None, :] < k[:, None])
    rank = jnp.sum(earlier.astype(jnp.int32), axis=1)
    code = key * cap + rank

    me = slab * reps + rep
    slot = jnp.arange(slabs * cap, dtype=jnp.int32)
    want = (((slot // cap) ^ slab) * (slabs * reps) + me) * cap + slot % cap
    send_ids = jnp.sum(
        jnp.where(code[None, :] == want[:, None], block_source[None, :] - me * stored, 0), axis=1
    )

    slot = jnp.arange(slabs * reps * cap, dtype=jnp.int32)
    dist = slot // (reps * cap)
    other = (slot // cap) % reps
    source = (dist ^ slab) * reps + (other ^ rep)
    want = (slab * (slabs * reps) + source) * cap + slot % cap
    hit = code[None, :] == want[:, None]
    v_ids = jnp.sum(jnp.where(hit, k[None, :] - slab * blk_dev, 0), axis=1)
    filled = jnp.sum(hit.astype(jnp.int32), axis=1)
    return send_ids, v_ids, filled


def row_range(height, part):
    first = height * SPLIT // 64 * 8
    return {None: (0, height), 0: (0, first), 1: (first, height - first)}[part]


def block_copy(t2_ref, number, out, sem, part=None):
    start = pl.multiple_of(number * BLK, BLK)
    low, size = row_range(t2_ref.shape[1], part)
    copy = pltpu.make_async_copy(
        t2_ref.at[:, pl.ds(low, size), pl.ds(start, BLK)], out, sem
    )
    copy.start()
    return copy


def block_shape(t2, blocks, part=None):
    size = row_range(t2.shape[1], part)[1]
    return jax.ShapeDtypeStruct((blocks, t2.shape[0], size, BLK), t2.dtype)


def flat(x):
    return x.reshape(x.shape[0], -1, BLK)


def pack_blocks(t2, send_ids, groups):
    total = sum(len(g) for g in groups)

    def body(ids, src, *rest):
        outs, sems = rest[:-1], rest[-1]
        copies = []
        for out, group in zip(outs, groups):
            for j, slot in enumerate(group):
                copies.append(block_copy(src, ids[slot], out.at[j], sems.at[len(copies)]))
        for copy in copies:
            copy.wait()

    packed = pl.pallas_call(
        body,
        out_shape=[block_shape(t2, len(g)) for g in groups],
        in_specs=[
            pl.BlockSpec(memory_space=pltpu.SMEM),
            pl.BlockSpec(memory_space=pltpu.HBM),
        ],
        out_specs=[pl.BlockSpec(memory_space=pltpu.VMEM)] * len(groups),
        scratch_shapes=[pltpu.SemaphoreType.DMA((total,))],
        compiler_params=pltpu.CompilerParams(vmem_limit_bytes=VMEM_LIMIT),
        cost_estimate=pl.CostEstimate(
            flops=0, bytes_accessed=2 * total * t2.shape[0] * t2.shape[1] * BLK * 4, transcendentals=0
        ),
        name="pack",
    )(send_ids, t2)
    return [flat(x) for x in packed]


def split(x):
    high = x.astype(jnp.bfloat16)
    return high, (x - high.astype(jnp.float32)).astype(jnp.bfloat16)


def dot(a, b):
    dims = (((1,), (1,)), ((), ()))
    return lax.dot_general(a, b, dims, preferred_element_type=jnp.float32)


def prepare(v, tables, slot_groups):
    _, v_ids, _ = tables
    cols = v.shape[0]
    total = sum(len(g) for g in slot_groups)

    def body(ids, v_ref, *refs):
        outs, (v_buf, sems) = refs[:-2], refs[-2:]
        copies = []
        for group in slot_groups:
            for slot in group:
                start = pl.multiple_of(ids[slot] * BLK, BLK)
                at = len(copies)
                copies.append(
                    pltpu.make_async_copy(
                        v_ref.at[:, pl.ds(start, BLK)], v_buf.at[at], sems.at[at]
                    )
                )
                copies[-1].start()
        n = 0
        for group, out in zip(slot_groups, outs):
            for j in range(len(group)):
                copies[n].wait()
                high, low = split(v_buf[n])
                out[:, pl.ds(j * BLK, BLK)] = high
                out[:, pl.ds((len(group) + j) * BLK, BLK)] = low
                n += 1

    return pl.pallas_call(
        body,
        out_shape=[
            jax.ShapeDtypeStruct((cols, 2 * len(g) * BLK), jnp.bfloat16) for g in slot_groups
        ],
        in_specs=[
            pl.BlockSpec(memory_space=pltpu.SMEM),
            pl.BlockSpec(memory_space=pltpu.HBM),
        ],
        out_specs=[pl.BlockSpec(memory_space=pltpu.VMEM)] * len(slot_groups),
        scratch_shapes=[
            pltpu.VMEM((total, cols, BLK), jnp.float32),
            pltpu.SemaphoreType.DMA((total,)),
        ],
        compiler_params=pltpu.CompilerParams(vmem_limit_bytes=VMEM_LIMIT),
        cost_estimate=pl.CostEstimate(
            flops=0, bytes_accessed=8 * total * cols * BLK, transcendentals=0
        ),
        name="prepare",
    )(v_ids, v)


def add_products(
    acc,
    parts,
    t2,
    v,
    tables,
    position,
    ready=None,
    turn=False,
    part=None,
    base=None,
    pass_on=0,
    fetch=(),
    cost=1,
):
    send_ids, v_ids, filled = tables
    where = [(i, n, slot) for i, (_, slots) in enumerate(parts) for n, slot in enumerate(slots)]
    slabs, height = t2.shape[:2]
    low, size = row_range(height, part)
    rows = slabs * size
    cols = v.shape[0]
    count = len(where)
    arrays = [x for x, _ in parts if x is not None]
    passed = sum(len(slots) for _, slots in parts[:pass_on])
    own = [n for n, (i, _, _) in enumerate(where) if parts[i][0] is None]
    fetched = len(own) + sum(len(g) for g, _ in fetch)
    results = 1 if base is None else slabs
    turned_here = turn or base is not None

    def body(*refs):
        refs = list(refs)
        ids, mask, sends, place, v_ref, t2_ref = refs[:6]
        del refs[:6]
        acc_ref = refs.pop(0) if acc is not None else None
        base_ref = refs.pop(0) if base is not None else None
        ready_ref = refs.pop(0) if ready is not None else None
        t_refs = [None if x is None else refs.pop(0) for x, _ in parts]
        v_buf, total, turned, v_sems, t_sems = refs[-5:]
        outs = refs[:-5]
        pass_ref = outs[results] if pass_on else None
        fetch_refs = outs[results + (pass_on > 0) :]

        v_copies, own_copies, late_copies = [], {}, []
        for n, (i, at, slot) in enumerate(where):
            if n in own:
                sem = t_sems.at[len(own_copies)]
                own_copies[n] = block_copy(t2_ref, sends[at], pass_ref.at[n], sem)
            if ready is not None:
                continue
            start = pl.multiple_of(ids[slot] * BLK, BLK)
            copy = pltpu.make_async_copy(v_ref.at[:, pl.ds(start, BLK)], v_buf.at[n], v_sems.at[n])
            copy.start()
            v_copies.append(copy)
        for (group, piece), out in zip(fetch, fetch_refs):
            for j, slot in enumerate(group):
                sem = t_sems.at[len(own) + len(late_copies)]
                late_copies.append(block_copy(t2_ref, sends[slot], out.at[j], sem, piece))

        def amplitudes(n):
            i, at, slot = where[n]
            if n in own:
                own_copies[n].wait()
                x = pass_ref[n].reshape(rows, BLK)
            else:
                x = t_refs[i][at]
            if filled is not None:
                x = jnp.where(mask[slot] > 0, x, 0.0)
            return x

        out_ref = total if turned_here else outs[0]
        depth = DEPTH if ready is None else count
        for n in range(0, count, depth):
            group = range(n, min(n + depth, count))
            t_high, t_low = split(jnp.concatenate([amplitudes(m) for m in group], axis=1))
            if ready is None:
                for m in group:
                    v_copies[m].wait()
                v_high, v_low = split(jnp.concatenate([v_buf[m] for m in group], axis=1))
                both = jnp.concatenate([v_high, v_low], axis=1)
            else:
                both, v_high = ready_ref[...], ready_ref[:, pl.ds(0, count * BLK)]
            product = dot(both, jnp.concatenate([t_high, t_high], axis=1)) + dot(v_high, t_low)
            if n > 0:
                out_ref[...] += product
            elif acc is None:
                out_ref[...] = product
            else:
                out_ref[...] = acc_ref[...] + product
        if turn:
            outs[0][...] = jnp.transpose(total[...])
        if base is not None:
            turned[...] = jnp.transpose(total[...])
            for d in range(slabs):
                owner = place[0] ^ d
                here = pl.multiple_of(owner * size, 8)
                there = pl.multiple_of(owner * height + low, 8)
                outs[d][...] = base_ref[pl.ds(there, size), :] + turned[pl.ds(here, size), :]
        for copy in late_copies:
            copy.wait()

    shapes = [(rows, cols) if turn else (cols, rows)] if base is None else [(size, cols)] * slabs
    out_shape = [jax.ShapeDtypeStruct(shape, jnp.float32) for shape in shapes]
    if pass_on:
        out_shape.append(block_shape(t2, passed))
    out_shape += [block_shape(t2, len(g), piece) for g, piece in fetch]
    whole = pl.BlockSpec(memory_space=pltpu.VMEM)
    operands = [v_ids, v_ids if filled is None else filled, send_ids, position, v, t2]
    specs = [pl.BlockSpec(memory_space=pltpu.SMEM)] * 4 + [pl.BlockSpec(memory_space=pltpu.HBM)] * 2
    if acc is not None:
        operands.append(acc)
        specs.append(whole)
    if base is not None:
        operands.append(base)
        specs.append(whole)
    if ready is not None:
        operands.append(ready)
        specs.append(whole)
    operands += arrays
    specs += [whole] * len(arrays)
    result = pl.pallas_call(
        body,
        out_shape=out_shape,
        in_specs=specs,
        out_specs=[whole] * len(out_shape),
        scratch_shapes=[
            pltpu.VMEM((count, cols, BLK) if ready is None else (1, 8, BLK), jnp.float32),
            pltpu.VMEM((cols, rows) if turned_here else (8, BLK), jnp.float32),
            pltpu.VMEM((8, BLK) if base is None else (rows, cols), jnp.float32),
            pltpu.SemaphoreType.DMA((count,)),
            pltpu.SemaphoreType.DMA((max(fetched, 1),)),
        ],
        compiler_params=pltpu.CompilerParams(vmem_limit_bytes=VMEM_LIMIT),
        cost_estimate=pl.CostEstimate(
            flops=6 * count * rows * cols * BLK * cost,
            bytes_accessed=4 * (count * BLK * (rows + cols) + 2 * rows * cols) * cost,
            transcendentals=0,
        ),
        name="products",
    )(*operands)
    return [*result[:results], *(flat(x) for x in result[results:])]


def cut(cap):
    size = min(CHUNK, cap // 2)
    edges = [*range(0, cap, size), cap]
    return list(zip(edges[:-1], edges[1:]))


def per_device(t2_stored, v_slab, block_source, r_in):
    slabs = lax.axis_size("slab")
    reps = lax.axis_size("rep")
    slab = lax.axis_index("slab")
    rep = lax.axis_index("rep")
    stored = t2_stored.shape[1] // BLK
    t2_stored = t2_stored.reshape(slabs, -1, t2_stored.shape[1])
    t2_stored = pltpu.with_memory_space_constraint(t2_stored, pltpu.HBM)
    blk_dev = v_slab.shape[1] // BLK
    cap = max(2, stored // slabs)
    send_ids, v_ids, filled = slot_tables(
        block_source, stored, blk_dev, cap, slabs, reps, slab, rep
    )
    v_ids = v_ids.reshape(slabs, reps, cap)
    filled = filled.reshape(slabs, reps, cap)
    if slabs * cap == stored:
        filled = None
    tables = (send_ids, v_ids, filled)
    position = jnp.stack([slab, rep]).astype(jnp.int32)

    def over_slab(x, d):
        return lax.ppermute(x, "slab", [(i, i ^ d) for i in range(slabs)])

    def over_rep(x, slots):
        return [
            (
                lax.ppermute(x, "rep", [(i, i ^ e) for i in range(reps)]),
                [(d, e, j) for d, _, j in slots],
            )
            for e in range(1, reps)
        ]

    def products(acc, parts, **kwargs):
        return add_products(acc, parts, t2_stored, v_slab, tables, position, **kwargs)

    spans = cut(cap)
    dists = range(slabs - 1, 0, -1)
    n = len(dists)
    end = len(spans) - 1

    def slots(c):
        return [[(d, 0, j) for j in range(*spans[c])] for d in dists]

    def places(c):
        groups = [[d * cap + j for d, _, j in g] for g in slots(c)] if c <= end else []
        return [(g, p) for p in ([0, 1] if c == end else [None]) for g in groups]

    def send(packed):
        return [over_slab(x, d) for x, d in zip(packed, [*dists] * 2)]

    def at_once(arrived, groups):
        return over_rep(jnp.concatenate(arrived, axis=0), [s for g in groups for s in g])

    packed = pack_blocks(t2_stored, send_ids, [g for g, _ in places(0)])
    landed = [send(packed)]
    packed, tables = lax.optimization_barrier((packed, tables))
    own_slots = [(0, 0, j) for j in range(cap)]
    acc, passed, *packed = products(None, [(None, own_slots)], pass_on=1, fetch=places(1), cost=COST)
    older = over_rep(passed, own_slots)
    ready = {}

    def prepare_ahead(c, acc):
        own = [s for g in slots(c) for s in g]
        others = [(d, e, j) for e in range(1, reps) for d, _, j in own]
        ids, acc = lax.optimization_barrier((v_ids, acc))
        blocks = prepare(v_slab, (send_ids, ids, filled), [own, others])
        ready[c], acc = lax.optimization_barrier((blocks, acc))
        return acc

    for c in range(end):
        if c + 1 == end:
            landed.append(send(packed[:n]))
            late = packed[n:]
        else:
            landed.append(send(packed))
        arrived, acc = lax.optimization_barrier((landed[c], acc))
        siblings = at_once(arrived, slots(c))
        acc, *packed = products(
            acc,
            list(zip(arrived, slots(c))),
            fetch=places(c + 2),
            ready=ready.get(c, (None,))[0],
            cost=COST,
        )
        if c + 1 == end:
            late, acc = lax.optimization_barrier((late, acc))
            landed.append(send(late))
        if c == 0:
            (acc,) = products(acc, older, cost=0)
        kwargs = {"ready": ready.get(c, (None, None))[1], "turn": c + 1 == end}
        (acc,) = products(acc, siblings, cost=0, **kwargs)
        if c == max(end - 3, 0) and end > 1:
            acc = prepare_ahead(end - 1, acc)
        if c == max(end - 2, 0):
            acc = prepare_ahead(end, acc)
    result = []
    for part in (0, 1):
        arrived, acc = lax.optimization_barrier((landed[end + part], acc))
        others = at_once(arrived, slots(end))
        first, second = ready[end]
        (sums,) = products(
            None, list(zip(arrived, slots(end))), ready=first, part=part, cost=PART_COST[part]
        )
        sums = products(
            sums, others, ready=second, base=acc, part=part, cost=COST * (1 - part)
        )
        sums, acc = lax.optimization_barrier((sums, acc))
        low, size = row_range(r_in.shape[0], part)
        own = r_in[low : low + size] + sums[0]
        for d in dists:
            own = own + over_slab(sums[d], d)
        result.append(own)
    return jnp.concatenate(result, axis=0)


def solution(mesh):
    in_specs = (P("row", ("slab", "rep")), P("rep", "slab"), P(), P(("row", "slab"), "rep"))
    out_specs = P(("row", "slab"), "rep")
    return jax.shard_map(
        per_device, mesh=mesh, in_specs=in_specs, out_specs=out_specs, check_vma=False
    )
```

```python
import jax
import jax.numpy as jnp
from jax import lax
from jax.experimental import pallas as pl
from jax.experimental.pallas import tpu as pltpu
from jax.sharding import PartitionSpec as P

BLK = 128
CHUNK = 2
COST = 20
PARTS = (0, 4, 6, 8)
PART_COST = (20, 20, 20)
DEPTH = 4
VMEM_LIMIT = 30 * 1024 * 1024


def slot_tables(block_source, stored, blk_dev, cap, slabs, reps, slab, rep):
    nblk = block_source.shape[0]
    k = jnp.arange(nblk, dtype=jnp.int32)
    holder = block_source // stored
    owner = k // blk_dev
    key = owner * (slabs * reps) + holder
    earlier = (key[None, :] == key[:, None]) & (k[None, :] < k[:, None])
    rank = jnp.sum(earlier.astype(jnp.int32), axis=1)
    code = key * cap + rank

    me = slab * reps + rep
    slot = jnp.arange(slabs * cap, dtype=jnp.int32)
    want = (((slot // cap) ^ slab) * (slabs * reps) + me) * cap + slot % cap
    send_ids = jnp.sum(
        jnp.where(code[None, :] == want[:, None], block_source[None, :] - me * stored, 0), axis=1
    )

    slot = jnp.arange(slabs * reps * cap, dtype=jnp.int32)
    dist = slot // (reps * cap)
    other = (slot // cap) % reps
    source = (dist ^ slab) * reps + (other ^ rep)
    want = (slab * (slabs * reps) + source) * cap + slot % cap
    hit = code[None, :] == want[:, None]
    v_ids = jnp.sum(jnp.where(hit, k[None, :] - slab * blk_dev, 0), axis=1)
    filled = jnp.sum(hit.astype(jnp.int32), axis=1)
    return send_ids, v_ids, filled


def row_range(height, part):
    if part is None:
        return 0, height
    low, high = (height * PARTS[i] // 64 * 8 for i in (part, part + 1))
    return low, high - low


def block_copy(t2_ref, number, out, sem, part=None):
    start = pl.multiple_of(number * BLK, BLK)
    low, size = row_range(t2_ref.shape[1], part)
    copy = pltpu.make_async_copy(
        t2_ref.at[:, pl.ds(low, size), pl.ds(start, BLK)], out, sem
    )
    copy.start()
    return copy


def block_shape(t2, blocks, part=None):
    size = row_range(t2.shape[1], part)[1]
    return jax.ShapeDtypeStruct((blocks, t2.shape[0], size, BLK), t2.dtype)


def flat(x):
    return x.reshape(x.shape[0], -1, BLK)


def pack_blocks(t2, send_ids, groups):
    total = sum(len(g) for g in groups)

    def body(ids, src, *rest):
        outs, sems = rest[:-1], rest[-1]
        copies = []
        for out, group in zip(outs, groups):
            for j, slot in enumerate(group):
                copies.append(block_copy(src, ids[slot], out.at[j], sems.at[len(copies)]))
        for copy in copies:
            copy.wait()

    packed = pl.pallas_call(
        body,
        out_shape=[block_shape(t2, len(g)) for g in groups],
        in_specs=[
            pl.BlockSpec(memory_space=pltpu.SMEM),
            pl.BlockSpec(memory_space=pltpu.HBM),
        ],
        out_specs=[pl.BlockSpec(memory_space=pltpu.VMEM)] * len(groups),
        scratch_shapes=[pltpu.SemaphoreType.DMA((total,))],
        compiler_params=pltpu.CompilerParams(vmem_limit_bytes=VMEM_LIMIT),
        cost_estimate=pl.CostEstimate(
            flops=0, bytes_accessed=2 * total * t2.shape[0] * t2.shape[1] * BLK * 4, transcendentals=0
        ),
        name="pack",
    )(send_ids, t2)
    return [flat(x) for x in packed]


def split(x):
    high = x.astype(jnp.bfloat16)
    return high, (x - high.astype(jnp.float32)).astype(jnp.bfloat16)


def dot(a, b):
    dims = (((1,), (1,)), ((), ()))
    return lax.dot_general(a, b, dims, preferred_element_type=jnp.float32)


def prepare(v, tables, slot_groups):
    _, v_ids, _ = tables
    cols = v.shape[0]
    total = sum(len(g) for g in slot_groups)

    def body(ids, v_ref, *refs):
        outs, (v_buf, sems) = refs[:-2], refs[-2:]
        copies = []
        for group in slot_groups:
            for slot in group:
                start = pl.multiple_of(ids[slot] * BLK, BLK)
                at = len(copies)
                copies.append(
                    pltpu.make_async_copy(
                        v_ref.at[:, pl.ds(start, BLK)], v_buf.at[at], sems.at[at]
                    )
                )
                copies[-1].start()
        n = 0
        for group, out in zip(slot_groups, outs):
            for j in range(len(group)):
                copies[n].wait()
                high, low = split(v_buf[n])
                out[:, pl.ds(j * BLK, BLK)] = high
                out[:, pl.ds((len(group) + j) * BLK, BLK)] = low
                n += 1

    return pl.pallas_call(
        body,
        out_shape=[
            jax.ShapeDtypeStruct((cols, 2 * len(g) * BLK), jnp.bfloat16) for g in slot_groups
        ],
        in_specs=[
            pl.BlockSpec(memory_space=pltpu.SMEM),
            pl.BlockSpec(memory_space=pltpu.HBM),
        ],
        out_specs=[pl.BlockSpec(memory_space=pltpu.VMEM)] * len(slot_groups),
        scratch_shapes=[
            pltpu.VMEM((total, cols, BLK), jnp.float32),
            pltpu.SemaphoreType.DMA((total,)),
        ],
        compiler_params=pltpu.CompilerParams(vmem_limit_bytes=VMEM_LIMIT),
        cost_estimate=pl.CostEstimate(
            flops=0, bytes_accessed=8 * total * cols * BLK, transcendentals=0
        ),
        name="prepare",
    )(v_ids, v)


def add_products(
    acc,
    parts,
    t2,
    v,
    tables,
    position,
    ready=None,
    turn=False,
    part=None,
    base=None,
    pass_on=0,
    fetch=(),
    cost=1,
):
    send_ids, v_ids, filled = tables
    where = [(i, n, slot) for i, (_, slots) in enumerate(parts) for n, slot in enumerate(slots)]
    slabs, height = t2.shape[:2]
    low, size = row_range(height, part)
    rows = slabs * size
    cols = v.shape[0]
    count = len(where)
    arrays = [x for x, _ in parts if x is not None]
    passed = sum(len(slots) for _, slots in parts[:pass_on])
    own = [n for n, (i, _, _) in enumerate(where) if parts[i][0] is None]
    fetched = len(own) + sum(len(g) for g, _ in fetch)
    results = 1 if base is None else slabs
    turned_here = turn or base is not None

    def body(*refs):
        refs = list(refs)
        ids, mask, sends, place, v_ref, t2_ref = refs[:6]
        del refs[:6]
        acc_ref = refs.pop(0) if acc is not None else None
        base_ref = refs.pop(0) if base is not None else None
        ready_ref = refs.pop(0) if ready is not None else None
        t_refs = [None if x is None else refs.pop(0) for x, _ in parts]
        v_buf, total, turned, v_sems, t_sems = refs[-5:]
        outs = refs[:-5]
        pass_ref = outs[results] if pass_on else None
        fetch_refs = outs[results + (pass_on > 0) :]

        v_copies, own_copies, late_copies = [], {}, []
        for n, (i, at, slot) in enumerate(where):
            if n in own:
                sem = t_sems.at[len(own_copies)]
                own_copies[n] = block_copy(t2_ref, sends[at], pass_ref.at[n], sem)
            if ready is not None:
                continue
            start = pl.multiple_of(ids[slot] * BLK, BLK)
            copy = pltpu.make_async_copy(v_ref.at[:, pl.ds(start, BLK)], v_buf.at[n], v_sems.at[n])
            copy.start()
            v_copies.append(copy)
        for (group, piece), out in zip(fetch, fetch_refs):
            for j, slot in enumerate(group):
                sem = t_sems.at[len(own) + len(late_copies)]
                late_copies.append(block_copy(t2_ref, sends[slot], out.at[j], sem, piece))

        def amplitudes(n):
            i, at, slot = where[n]
            if n in own:
                own_copies[n].wait()
                x = pass_ref[n].reshape(rows, BLK)
            else:
                x = t_refs[i][at]
            if filled is not None:
                x = jnp.where(mask[slot] > 0, x, 0.0)
            return x

        out_ref = total if turned_here else outs[0]
        depth = DEPTH if ready is None else count
        for n in range(0, count, depth):
            group = range(n, min(n + depth, count))
            t_high, t_low = split(jnp.concatenate([amplitudes(m) for m in group], axis=1))
            if ready is None:
                for m in group:
                    v_copies[m].wait()
                v_high, v_low = split(jnp.concatenate([v_buf[m] for m in group], axis=1))
                both = jnp.concatenate([v_high, v_low], axis=1)
            else:
                both, v_high = ready_ref[...], ready_ref[:, pl.ds(0, count * BLK)]
            product = dot(both, jnp.concatenate([t_high, t_high], axis=1)) + dot(v_high, t_low)
            if n > 0:
                out_ref[...] += product
            elif acc is None:
                out_ref[...] = product
            else:
                out_ref[...] = acc_ref[...] + product
        if turn:
            outs[0][...] = jnp.transpose(total[...])
        if base is not None:
            turned[...] = jnp.transpose(total[...])
            for d in range(slabs):
                owner = place[0] ^ d
                here = pl.multiple_of(owner * size, 8)
                there = pl.multiple_of(owner * height + low, 8)
                outs[d][...] = base_ref[pl.ds(there, size), :] + turned[pl.ds(here, size), :]
        for copy in late_copies:
            copy.wait()

    shapes = [(rows, cols) if turn else (cols, rows)] if base is None else [(size, cols)] * slabs
    out_shape = [jax.ShapeDtypeStruct(shape, jnp.float32) for shape in shapes]
    if pass_on:
        out_shape.append(block_shape(t2, passed))
    out_shape += [block_shape(t2, len(g), piece) for g, piece in fetch]
    whole = pl.BlockSpec(memory_space=pltpu.VMEM)
    operands = [v_ids, v_ids if filled is None else filled, send_ids, position, v, t2]
    specs = [pl.BlockSpec(memory_space=pltpu.SMEM)] * 4 + [pl.BlockSpec(memory_space=pltpu.HBM)] * 2
    if acc is not None:
        operands.append(acc)
        specs.append(whole)
    if base is not None:
        operands.append(base)
        specs.append(whole)
    if ready is not None:
        operands.append(ready)
        specs.append(whole)
    operands += arrays
    specs += [whole] * len(arrays)
    result = pl.pallas_call(
        body,
        out_shape=out_shape,
        in_specs=specs,
        out_specs=[whole] * len(out_shape),
        scratch_shapes=[
            pltpu.VMEM((count, cols, BLK) if ready is None else (1, 8, BLK), jnp.float32),
            pltpu.VMEM((cols, rows) if turned_here else (8, BLK), jnp.float32),
            pltpu.VMEM((8, BLK) if base is None else (rows, cols), jnp.float32),
            pltpu.SemaphoreType.DMA((count,)),
            pltpu.SemaphoreType.DMA((max(fetched, 1),)),
        ],
        compiler_params=pltpu.CompilerParams(vmem_limit_bytes=VMEM_LIMIT),
        cost_estimate=pl.CostEstimate(
            flops=6 * count * rows * cols * BLK * cost,
            bytes_accessed=4 * (count * BLK * (rows + cols) + 2 * rows * cols) * cost,
            transcendentals=0,
        ),
        name="products",
    )(*operands)
    return [*result[:results], *(flat(x) for x in result[results:])]


def cut(cap):
    size = min(CHUNK, cap // 2)
    edges = [*range(0, cap, size), cap]
    return list(zip(edges[:-1], edges[1:]))


def per_device(t2_stored, v_slab, block_source, r_in):
    slabs = lax.axis_size("slab")
    reps = lax.axis_size("rep")
    slab = lax.axis_index("slab")
    rep = lax.axis_index("rep")
    stored = t2_stored.shape[1] // BLK
    t2_stored = t2_stored.reshape(slabs, -1, t2_stored.shape[1])
    t2_stored = pltpu.with_memory_space_constraint(t2_stored, pltpu.HBM)
    blk_dev = v_slab.shape[1] // BLK
    cap = max(2, stored // slabs)
    send_ids, v_ids, filled = slot_tables(
        block_source, stored, blk_dev, cap, slabs, reps, slab, rep
    )
    v_ids = v_ids.reshape(slabs, reps, cap)
    filled = filled.reshape(slabs, reps, cap)
    if slabs * cap == stored:
        filled = None
    tables = (send_ids, v_ids, filled)
    position = jnp.stack([slab, rep]).astype(jnp.int32)

    def over_slab(x, d):
        return lax.ppermute(x, "slab", [(i, i ^ d) for i in range(slabs)])

    def over_rep(x, slots):
        return [
            (
                lax.ppermute(x, "rep", [(i, i ^ e) for i in range(reps)]),
                [(d, e, j) for d, _, j in slots],
            )
            for e in range(1, reps)
        ]

    def products(acc, parts, **kwargs):
        return add_products(acc, parts, t2_stored, v_slab, tables, position, **kwargs)

    spans = cut(cap)
    dists = range(slabs - 1, 0, -1)
    n = len(dists)
    end = len(spans) - 1

    def slots(c):
        return [[(d, 0, j) for j in range(*spans[c])] for d in dists]

    def places(c):
        groups = [[d * cap + j for d, _, j in g] for g in slots(c)] if c <= end else []
        return [(g, p) for p in (range(len(PARTS) - 1) if c == end else [None]) for g in groups]

    def send(packed):
        return [over_slab(x, d) for x, d in zip(packed, dists)]

    def at_once(arrived, groups):
        return over_rep(jnp.concatenate(arrived, axis=0), [s for g in groups for s in g])

    packed = pack_blocks(t2_stored, send_ids, [g for g, _ in places(0)])
    landed = [send(packed)]
    packed, tables = lax.optimization_barrier((packed, tables))
    own_slots = [(0, 0, j) for j in range(cap)]
    acc, passed, *packed = products(None, [(None, own_slots)], pass_on=1, fetch=places(1), cost=COST)
    older = over_rep(passed, own_slots)
    ready = {}

    def prepare_ahead(c, acc):
        own = [s for g in slots(c) for s in g]
        others = [(d, e, j) for e in range(1, reps) for d, _, j in own]
        ids, acc = lax.optimization_barrier((v_ids, acc))
        blocks = prepare(v_slab, (send_ids, ids, filled), [own, others])
        ready[c], acc = lax.optimization_barrier((blocks, acc))
        return acc

    for c in range(end):
        if c + 1 == end:
            landed.append(send(packed[:n]))
            late = packed[n:]
        else:
            landed.append(send(packed))
        arrived, acc = lax.optimization_barrier((landed[c], acc))
        siblings = at_once(arrived, slots(c))
        acc, *packed = products(
            acc,
            list(zip(arrived, slots(c))),
            fetch=places(c + 2),
            ready=ready.get(c, (None,))[0],
            cost=COST,
        )
        if c + 1 == end:
            next_part, acc = lax.optimization_barrier((late[:n], acc))
            landed.append(send(next_part))
            late = late[n:]
        if c == 0:
            (acc,) = products(acc, older, cost=0)
        kwargs = {"ready": ready.get(c, (None, None))[1], "turn": c + 1 == end}
        (acc,) = products(acc, siblings, cost=0, **kwargs)
        if c == max(end - 3, 0) and end > 1:
            acc = prepare_ahead(end - 1, acc)
        if c == max(end - 2, 0):
            acc = prepare_ahead(end, acc)
    result = []
    for part in range(len(PARTS) - 1):
        if late:
            next_part, acc = lax.optimization_barrier((late[:n], acc))
            landed.append(send(next_part))
            late = late[n:]
        arrived, acc = lax.optimization_barrier((landed[end + part], acc))
        others = at_once(arrived, slots(end))
        first, second = ready[end]
        (sums,) = products(
            None, list(zip(arrived, slots(end))), ready=first, part=part, cost=PART_COST[part]
        )
        sums = products(
            sums, others, ready=second, base=acc, part=part, cost=PART_COST[part]
        )
        sums, acc = lax.optimization_barrier((sums, acc))
        low, size = row_range(r_in.shape[0], part)
        own = r_in[low : low + size] + sums[0]
        for d in dists:
            own = own + over_slab(sums[d], d)
        result.append(own)
    return jnp.concatenate(result, axis=0)


def solution(mesh):
    in_specs = (P("row", ("slab", "rep")), P("rep", "slab"), P(), P(("row", "slab"), "rep"))
    out_specs = P(("row", "slab"), "rep")
    return jax.shard_map(
        per_device, mesh=mesh, in_specs=in_specs, out_specs=out_specs, check_vma=False
    )
```
